256 devices in a mesh: feat: 16 (over x, y), group: 8 (over z), rep: 2 (over core).
Axes of the slice: x: 4, y: 4, z: 8, core: 2. Of those that a mesh axis runs over, the one named last changes fastest.
Arguments:
- seed_feats: bfloat16 [65536, 768], P(('rep', 'group'), 'feat'), parts along dimension 0, may hold values from -6 to 6
- src_feats: bfloat16 [131072, 768], P(('rep', 'group'), 'feat'), parts along dimension 0, may hold values from -6 to 6
- counts: int32 [1536, 128, 128], P(('rep', 'group')), parts along dimension 0, may hold values from 0 to 3, as said below
- dst_block: int32 [1536], P(('rep', 'group')), parts along dimension 0, may hold values from 0 to 255
- src_block: int32 [1536], P(('rep', 'group')), parts along dimension 0, may hold values from 0 to 63
- w_self: bfloat16 [768, 1024], replicated, may hold values from -0.21875 to 0.21875
- w_neigh: bfloat16 [768, 1024], replicated, may hold values from -0.21875 to 0.21875
- cotangent: bfloat16 [65536, 1024], P(('rep', 'group'), 'feat'), parts along dimension 0, may hold values from -6 to 6
Outputs:
- hidden: bfloat16 [65536, 1024], P(('rep', 'group'), 'feat'), parts along dimension 0
- grad_self: float32 [1536, 1024], P(('rep', 'feat'), 'group'), parts along dimension 0
- grad_neigh: float32 [1536, 1024], P(('rep', 'feat'), 'group'), parts along dimension 0
The draws below stay inside these ranges and needn't reach their ends.
There are 2 independent parts, one for each index of `rep`. The reference program is written for one: setup_inputs(seed, part) draws one part's arguments, and reference() takes and returns one part's arrays. A program takes and returns all parts, laid end to end along the dimension named above; an argument that names none is the same for every part. Nothing has to cross between parts.
Inputs may be any that keep to these rules, and one draw needn't show every extreme that they name: Small edge counts; tiles are sparse.
All inputs are finite; a program needn't handle non-finite values.
Results may differ from the reference program's by a relative error of at most 0.013.
The reference program's roundings to bfloat16 on the way (of `neigh_mean` and `dpre`) count: a program that leaves them out, or rounds other values in their place, can miss the bound.
Values may be sent and summed in bfloat16 or wider, within the bound.
No kernel may reach another device: no remote copies, remote signals or barrier semaphores. Data moves between devices by JAX's collectives and lax.ppermute only.
A program may use at most 128 MiB of HBM per device.

```python
import math
import jax
import jax.numpy as jnp
import numpy as np

D = 768
HID = 1024
TILE = 128
SRC_GRP = 8192
TILES_GRP = 96
SEEDS = 32768
SOURCES = 65536
TILES = 768
N_GROUP = 8


def draw_counts(key, part):
    key = jax.random.fold_in(key, 5)
    key_val, key_keep = jax.random.split(key)
    values = jax.random.randint(key_val, (TILES, TILE, TILE), 1, 4)
    chance = jax.random.randint(key_keep, (TILES, TILE, TILE), 0, 1000)
    groups = TILES // TILES_GRP
    owner = jnp.arange(TILES, dtype=jnp.int32) // TILES_GRP
    limit = 40 + 80 * owner // max(groups - 1, 1)
    return jnp.where(chance < limit[:, None, None], values, 0).astype(jnp.int32)


def set_ends(entries, rng, low, high):
    longest = entries.shape.index(max(entries.shape))
    spots = []
    for shift in (0, 1):
        where = [jax.random.randint(jax.random.fold_in(rng, axis), (), 0, length) for axis, length in enumerate(entries.shape)]
        where[longest] = (where[longest] + shift) % entries.shape[longest]
        spots.append(tuple(where))
    return entries.at[spots[0]].set(low).at[spots[1]].set(high)


def level_of(own_key, shape, cuts, smallest, largest):
    factor_of = 1.0
    for dim, blocks in cuts:
        steps = jax.random.uniform(jax.random.fold_in(jax.random.fold_in(own_key, 6), dim), (blocks,), jnp.float32, smallest / len(cuts), largest / len(cuts))
        factor_of = factor_of * jnp.repeat(jnp.exp(steps), shape[dim] // blocks).reshape((-1,) + (1,) * (len(shape) - 1 - dim))
    return factor_of


def rank_table(count, slope):
    portions = [(1 << 20) // math.isqrt(rank ** slope) + 1 for rank in range(1, count + 1)]
    spread = 1 + sum(portions) // (1 << 30)
    return np.cumsum(np.array([max(1, weight // spread) for weight in portions]))


def skewed_ids(own_key, extent, count, skew):
    grid = rank_table(count, skew)
    lot = jax.random.randint(jax.random.fold_in(own_key, 1), extent, 0, int(grid[count - 1]))
    rank = jnp.searchsorted(jnp.asarray(grid, jnp.int32), lot, side="right")
    return jax.random.permutation(jax.random.fold_in(own_key, 2), count)[rank].astype(jnp.int32)


def noise(stream_key, shape, spread, most, cuts=(), kind=jnp.bfloat16):
    array = jax.random.normal(stream_key, shape, jnp.float32) * spread
    if len(cuts) > 0:
        array = level_of(stream_key, shape, cuts, -0.22, 0.18) * array
    return jnp.clip(array, min=-most, max=most).astype(kind)


def setup_inputs(seed: int = 0, part: int = 0) -> dict:
    arg_keys = jax.random.split(jax.random.key(seed), 9)
    own_keys = jax.random.split(jax.random.fold_in(arg_keys[8], part), 9)
    seed_feats = noise(own_keys[0], (SEEDS, D), 1.0, 6.0, ((0, 8), (1, 16)))
    src_feats = noise(own_keys[1], (SOURCES, D), 1.0, 6.0, ((0, 8), (1, 16)))
    counts = draw_counts(jax.random.fold_in(jax.random.fold_in(arg_keys[8], part), 71), part)
    dst_block = set_ends(skewed_ids(own_keys[3], (TILES,), SEEDS // TILE, 2), jax.random.fold_in(own_keys[3], 3), 0, (SEEDS // TILE) - 1).astype(jnp.int32)
    src_block = set_ends(jax.random.randint(own_keys[4], (TILES,), 0, SRC_GRP // TILE), jax.random.fold_in(own_keys[4], 1), 0, (SRC_GRP // TILE) - 1).astype(jnp.int32)
    w_self = noise(arg_keys[5], (D, HID), D ** -0.5, 0.21875)
    w_neigh = noise(arg_keys[6], (D, HID), D ** -0.5, 0.21875)
    cotangent = noise(own_keys[7], (SEEDS, HID), 1.0, 6.0, ((0, 8), (1, 16)))
    return {"seed_feats": seed_feats, "src_feats": src_feats, "counts": counts, "dst_block": dst_block, "src_block": src_block, "w_self": w_self, "w_neigh": w_neigh, "cotangent": cotangent}


def reference(seed_feats, src_feats, counts, dst_block, src_block, w_self, w_neigh, cotangent):
    tile = counts.shape[1]
    width = seed_feats.shape[1]
    nblk = seed_feats.shape[0] // tile
    per_group = src_feats.shape[0] // N_GROUP // tile
    owner = jnp.arange(counts.shape[0], dtype=jnp.int32) // (counts.shape[0] // N_GROUP)
    global_blk = (owner * per_group + src_block).astype(jnp.int32)
    blocks = src_feats.reshape(-1, tile, width)[global_blk]
    tile_out = jnp.einsum("tij,tjf->tif", counts.astype(jnp.float32), blocks.astype(jnp.float32))
    neigh_sum = jax.ops.segment_sum(tile_out, dst_block, nblk).reshape(-1, width)
    degree = jax.ops.segment_sum(jnp.sum(counts, axis=2).astype(jnp.float32), dst_block, nblk).reshape(-1)
    neigh_mean = (neigh_sum / (degree[:, None] + 1.0)).astype(jnp.bfloat16)
    pre = jnp.dot(seed_feats, w_self, preferred_element_type=jnp.float32) + jnp.dot(neigh_mean, w_neigh, preferred_element_type=jnp.float32)
    hidden = jnp.maximum(pre, 0.0).astype(jnp.bfloat16)
    dpre = jnp.where(hidden > 0, cotangent, jnp.zeros_like(cotangent))
    grad_self = jnp.dot(seed_feats.T, dpre, preferred_element_type=jnp.float32)
    grad_neigh = jnp.dot(neigh_mean.T, dpre, preferred_element_type=jnp.float32)
    return hidden, grad_self, grad_neigh
```

```python
import jax
import jax.numpy as jnp
from jax import lax
from jax.experimental import pallas as pl
from jax.experimental.pallas import tpu as pltpu
from jax.sharding import PartitionSpec as P

F32, BF16 = jnp.float32, jnp.bfloat16
UNROLL = 16
SIDE = 4
HBM = pl.BlockSpec(memory_space=pltpu.HBM)


def far(*arrays):
    return [pltpu.with_memory_space_constraint(a, pltpu.HBM) for a in arrays]


def tile_kernel(dst_ref, src_ref, feats_h, counts_ref, acc, deg_ref, held, feats, sem):
    step = pl.program_id(0)
    cols = feats.shape[0]
    nsrc, rows, tile = held.shape
    per_owner = acc.shape[2] // tile

    @pl.when(step == 0)
    def _():
        load = pltpu.make_async_copy(feats_h, feats, sem)
        load.start()
        acc[...] = jnp.zeros_like(acc)
        deg_ref[...] = jnp.zeros_like(deg_ref)
        load.wait()
        for b in range(nsrc):
            held[b, :cols, :] = feats[:, b * tile : (b + 1) * tile]
            held[b, cols:, :] = jnp.ones((rows - cols, tile), BF16)

    for u in range(UNROLL):
        t = step * UNROLL + u
        d = dst_ref[t]
        got = lax.dot_general(
            held[src_ref[t]],
            counts_ref[u].astype(F32).astype(BF16),
            (((1,), (1,)), ((), ())),
            preferred_element_type=F32,
        )
        owner = d // per_owner
        lanes = pl.ds(pl.multiple_of((d % per_owner) * tile, tile), tile)
        acc[owner, :, lanes] += got[:cols]
        deg_ref[owner, :, lanes] += got[cols : cols + 8]


def tile_sums(dst_block, src_block, feats_t, counts, owners, seeds_here):
    ntile, tile, _ = counts.shape
    cols, sources = feats_t.shape
    outs = [(owners, cols, seeds_here), (owners, 8, seeds_here)]
    return pl.pallas_call(
        tile_kernel,
        grid_spec=pltpu.PrefetchScalarGridSpec(
            num_scalar_prefetch=2,
            grid=(ntile // UNROLL,),
            in_specs=[HBM, pl.BlockSpec((UNROLL, tile, tile), lambda i, *_: (i, 0, 0))],
            out_specs=[pl.BlockSpec(o, lambda i, *_: (0, 0, 0)) for o in outs],
            scratch_shapes=[
                pltpu.VMEM((sources // tile, cols + 16, tile), BF16),
                pltpu.VMEM((cols, sources), BF16),
                pltpu.SemaphoreType.DMA,
            ],
        ),
        out_shape=[pltpu.HBM(o, F32) for o in outs],
        compiler_params=pltpu.CompilerParams(
            dimension_semantics=("arbitrary",), vmem_limit_bytes=48 * 1024 * 1024
        ),
    )(*far(dst_block, src_block, feats_t), counts)


def mean_kernel(total_h, degree_h, send_h, total, degree, send, sems):
    loads = [
        pltpu.make_async_copy(total_h, total, sems.at[0]),
        pltpu.make_async_copy(degree_h, degree, sems.at[1]),
    ]
    for load in loads:
        load.start()
    for load in loads:
        load.wait()
    width = send.shape[2]
    stores = []
    for y in range(SIDE):
        lanes = slice(y * width, (y + 1) * width)
        send[y] = (total[:, lanes] / (degree[:, lanes] + 1.0)).astype(BF16)
    for x in range(SIDE):
        store = pltpu.make_async_copy(send, send_h.at[pl.ds(x * SIDE, SIDE)], sems.at[2 + x])
        store.start()
        stores.append(store)
    for store in stores:
        store.wait()


def mean_rows(total, degree):
    cols, n = total.shape
    send = (SIDE, cols, n // SIDE)
    return pl.pallas_call(
        mean_kernel,
        in_specs=[HBM, HBM],
        out_specs=HBM,
        out_shape=pltpu.HBM((SIDE * SIDE, *send[1:]), BF16),
        scratch_shapes=[
            pltpu.VMEM(total.shape, F32),
            pltpu.VMEM(degree.shape, F32),
            pltpu.VMEM(send, BF16),
            pltpu.SemaphoreType.DMA((2 + SIDE,)),
        ],
        compiler_params=pltpu.CompilerParams(vmem_limit_bytes=16 * 1024 * 1024),
    )(*far(total), degree)


def layer_kernel(wn_h, means_h, pre_h, cot_h, seeds_h, hid_h, grad_h, *refs):
    wn, means, pre, cot, seeds, hid, grad, sems = refs
    given = (wn_h, means_h, pre_h, cot_h, seeds_h)
    near = (wn, means, pre, cot, seeds)
    loads = [pltpu.make_async_copy(given[i], near[i], sems.at[i]) for i in range(5)]
    for load in loads:
        load.start()
    nf, rows, _ = grad.shape
    cols = rows // 2
    for load in loads[:3]:
        load.wait()
    total = pre[...] + jnp.dot(wn[...], means[...], preferred_element_type=F32)
    h = jnp.maximum(total, 0.0).astype(BF16)
    hid[...] = h
    stores = [pltpu.make_async_copy(hid, hid_h, sems.at[5])]
    stores[0].start()
    loads[3].wait()
    dpre = jnp.where(h > 0, cot[...], jnp.zeros_like(h))
    dims = (((1,), (1,)), ((), ()))
    loads[4].wait()
    for j, x in enumerate((means, seeds)):
        at = (1 - j) * cols
        g = lax.dot_general(x[...], dpre, dims, preferred_element_type=F32).astype(BF16)
        for i in range(nf):
            grad[i, at : at + cols, :] = g[i * cols : (i + 1) * cols]
        where = (slice(None), pl.ds(at, cols), slice(None))
        store = pltpu.make_async_copy(grad.at[where], grad_h.at[where], sems.at[6 + j])
        store.start()
        stores.append(store)
    for store in stores:
        store.wait()


def layer(wn_t, means, pre_self, cot, seeds, nf):
    hcols, rows = pre_self.shape
    args = (wn_t, means, pre_self, cot, seeds)
    shapes = [(hcols, rows), (nf, 2 * means.shape[0] // nf, hcols)]
    return pl.pallas_call(
        layer_kernel,
        in_specs=[HBM] * 5,
        out_specs=[HBM] * 2,
        out_shape=[pltpu.HBM(o, BF16) for o in shapes],
        scratch_shapes=[pltpu.VMEM(a.shape, a.dtype) for a in args]
        + [pltpu.VMEM(o, BF16) for o in shapes]
        + [pltpu.SemaphoreType.DMA((8,))],
        compiler_params=pltpu.CompilerParams(vmem_limit_bytes=40 * 1024 * 1024),
    )(*far(*args))


def shards(seed_feats, src_feats, counts, dst_block, src_block, w_self, w_neigh, cotangent):
    seeds_here, cols = seed_feats.shape
    ng = lax.axis_size("group")
    nf = lax.axis_size("feat")
    part = seeds_here // SIDE
    ccols = cotangent.shape[1]
    hcols = SIDE * ccols
    f = lax.axis_index("feat")
    fx, fy = f // SIDE, f % SIDE
    along_y = [[x * SIDE + y for y in range(SIDE)] for x in range(SIDE)]

    def shift_y(a, k):
        return lax.ppermute(
            a, "feat", [(i, i // SIDE * SIDE + (i % SIDE + k) % SIDE) for i in range(nf)]
        )

    with jax.named_scope("tile_sums"):
        sums, deg = tile_sums(dst_block, src_block, src_feats.T, counts, ng, seeds_here)

    with jax.named_scope("neighbour_sum"):
        total = lax.psum_scatter(
            sums.reshape(ng * cols, seeds_here), "group", scatter_dimension=0, tiled=True
        )

    seed_t, cot_t, deg, _ = lax.optimization_barrier((seed_feats.T, cotangent.T, deg, sums))

    with jax.named_scope("degree"):
        degree = jnp.sum(lax.all_to_all(deg[:, 0], "group", 0, 0, tiled=True), axis=0)[None]

    with jax.named_scope("cotangent_rows"):
        send = cot_t.reshape(ccols, SIDE, part).transpose(1, 0, 2)
        cot = lax.all_to_all(send, "feat", 0, 0, axis_index_groups=along_y)
        cot = cot.reshape(hcols, part)

    with jax.named_scope("seed_rows"):
        send = seed_t.reshape(cols, SIDE, part).transpose(1, 0, 2)
        send = jnp.broadcast_to(send[None], (SIDE, SIDE, cols, part)).reshape(nf, cols, part)
        seeds = lax.all_to_all(send, "feat", 0, 0).reshape(nf * cols, part)

    with jax.named_scope("self_part"):
        ws_t = lax.dynamic_slice_in_dim(w_self, fx * hcols, hcols, 1).T
        wn_t = lax.dynamic_slice_in_dim(w_neigh, fx * hcols, hcols, 1).T
        pre_self = jnp.dot(ws_t, seeds, preferred_element_type=F32)

    with jax.named_scope("mean_rows"):
        total, degree, pre_self, cot = lax.optimization_barrier((total, degree, pre_self, cot))
        send = mean_rows(total, degree)
        means = lax.all_to_all(send, "feat", 0, 0).reshape(nf * cols, part)

    with jax.named_scope("layer"):
        hid, both = layer(wn_t, means, pre_self, cot, seeds, nf)

    with jax.named_scope("grads"):
        got = lax.all_to_all(both, "feat", 0, 0).astype(F32)
        got = jnp.sum(got.reshape(SIDE, SIDE, 2 * cols, hcols), axis=1)
        got = got.reshape(SIDE, 2 * cols, 2, hcols // 2).transpose(0, 2, 1, 3)
        got = got.reshape(ng, 2 * cols, hcols // 2).astype(BF16)
        got, hid = lax.optimization_barrier((got, hid))
        got = jnp.sum(lax.all_to_all(got, "group", 0, 0).astype(F32), axis=0)

    with jax.named_scope("hidden_columns"):
        hid4 = hid.reshape(SIDE, ccols, part)
        out = jnp.zeros((ccols, seeds_here), BF16)
        for k in range(SIDE):
            piece = lax.dynamic_index_in_dim(hid4, (fy + k) % SIDE, 0, keepdims=False)
            piece = shift_y(piece, k) if k else piece
            out = lax.dynamic_update_slice(out, piece, (0, (fy - k) % SIDE * part))
    return (out.T, got[:cols], got[cols:])


def solution(mesh):
    in_specs = (
        P(("rep", "group"), "feat"),
        P(("rep", "group"), "feat"),
        P(("rep", "group"), None, None),
        P(("rep", "group")),
        P(("rep", "group")),
        P(),
        P(),
        P(("rep", "group"), "feat"),
    )
    out_specs = (
        P(("rep", "group"), "feat"),
        P(("rep", "feat"), "group"),
        P(("rep", "feat"), "group"),
    )
    return jax.shard_map(shards, mesh=mesh, in_specs=in_specs, out_specs=out_specs, check_vma=False)
```

```python
import jax
import jax.numpy as jnp
from jax import lax
from jax.experimental import pallas as pl
from jax.experimental.pallas import tpu as pltpu
from jax.sharding import PartitionSpec as P

F32, BF16 = jnp.float32, jnp.bfloat16
UNROLL = 16
SIDE = 4
HBM = pl.BlockSpec(memory_space=pltpu.HBM)


def far(*arrays):
    return [pltpu.with_memory_space_constraint(a, pltpu.HBM) for a in arrays]


def tile_kernel(dst_h, src_h, feats_h, counts_h, sums_h, deg_h, *refs):
    dst, src, feats, counts, acc, deg, held, sems = refs
    cols = feats.shape[0]
    nsrc, rows, tile = held.shape
    owners, _, seeds_here = acc.shape
    per_owner = seeds_here // tile
    ntile = counts.shape[0]
    nload = ntile // UNROLL

    def load_counts(c):
        where = pl.ds(c * UNROLL, UNROLL)
        return pltpu.make_async_copy(counts_h.at[where], counts.at[where], sems.at[c])

    loads = [
        pltpu.make_async_copy(dst_h, dst, sems.at[nload]),
        pltpu.make_async_copy(src_h, src, sems.at[nload + 1]),
        pltpu.make_async_copy(feats_h, feats, sems.at[nload + 2]),
    ]
    for load in loads:
        load.start()
    for c in range(nload):
        load_counts(c).start()
    acc[...] = jnp.zeros_like(acc)
    deg[...] = jnp.zeros_like(deg)
    held[:, cols:, :] = jnp.ones((nsrc, rows - cols, tile), BF16)
    for load in loads:
        load.wait()
    for b in range(nsrc):
        held[b, :cols, :] = feats[:, b * tile : (b + 1) * tile]

    def chunk(c, _):
        load_counts(c).wait()
        for u in range(UNROLL):
            t = c * UNROLL + u
            d = dst[t]
            got = lax.dot_general(
                held[src[t]],
                counts[t].astype(F32).astype(BF16),
                (((1,), (1,)), ((), ())),
                preferred_element_type=F32,
            )
            owner = d // per_owner
            lanes = pl.ds(pl.multiple_of((d % per_owner) * tile, tile), tile)
            acc[owner, :, lanes] += got[:cols]
            deg[owner, :, lanes] += got[cols : cols + 8]
        return _

    lax.fori_loop(0, nload, chunk, 0)
    stores = [
        pltpu.make_async_copy(acc, sums_h, sems.at[0]),
        pltpu.make_async_copy(deg, deg_h, sems.at[1]),
    ]
    for store in stores:
        store.start()
    for store in stores:
        store.wait()


def tile_sums(dst_block, src_block, feats_t, counts, owners, seeds_here):
    ntile, tile, _ = counts.shape
    cols, sources = feats_t.shape
    outs = [(owners, cols, seeds_here), (owners, 8, seeds_here)]
    return pl.pallas_call(
        tile_kernel,
        in_specs=[HBM] * 4,
        out_specs=[HBM] * 2,
        out_shape=[pltpu.HBM(o, F32) for o in outs],
        scratch_shapes=[
            pltpu.SMEM((ntile,), jnp.int32),
            pltpu.SMEM((ntile,), jnp.int32),
            pltpu.VMEM((cols, sources), BF16),
            pltpu.VMEM(counts.shape, jnp.int32),
            *[pltpu.VMEM(o, F32) for o in outs],
            pltpu.VMEM((sources // tile, cols + 16, tile), BF16),
            pltpu.SemaphoreType.DMA((ntile // UNROLL + 3,)),
        ],
        compiler_params=pltpu.CompilerParams(vmem_limit_bytes=40 * 1024 * 1024),
    )(*far(dst_block, src_block, feats_t, counts))


def mean_kernel(total_h, degree_h, send_h, total, degree, send, sems):
    width = send.shape[2]
    lanes = [pl.ds(y * width, width) for y in range(SIDE)]
    first = pltpu.make_async_copy(degree_h, degree, sems.at[0])
    first.start()
    loads = [
        pltpu.make_async_copy(total_h.at[:, lanes[y]], total.at[:, lanes[y]], sems.at[1 + y])
        for y in range(SIDE)
    ]
    for load in loads:
        load.start()
    first.wait()
    stores = []
    for y in range(SIDE):
        loads[y].wait()
        send[y] = (total[:, lanes[y]] / (degree[:, lanes[y]] + 1.0)).astype(BF16)
        for x in range(SIDE):
            i = x * SIDE + y
            store = pltpu.make_async_copy(send.at[y], send_h.at[i], sems.at[1 + SIDE + i])
            store.start()
            stores.append(store)
    for store in stores:
        store.wait()


def mean_rows(total, degree):
    cols, n = total.shape
    send = (SIDE, cols, n // SIDE)
    return pl.pallas_call(
        mean_kernel,
        in_specs=[HBM, HBM],
        out_specs=HBM,
        out_shape=pltpu.HBM((SIDE * SIDE, *send[1:]), BF16),
        scratch_shapes=[
            pltpu.VMEM(total.shape, F32),
            pltpu.VMEM(degree.shape, F32),
            pltpu.VMEM(send, BF16),
            pltpu.SemaphoreType.DMA((1 + SIDE + SIDE * SIDE,)),
        ],
        compiler_params=pltpu.CompilerParams(vmem_limit_bytes=16 * 1024 * 1024),
    )(*far(total), degree)


def layer_kernel(ws_h, seeds_h, wn_h, means_h, cot_h, hid_h, grad_h, *refs):
    ws, seeds, wn, means, cot, hid, grad, sems = refs
    given = (ws_h, seeds_h, wn_h, means_h, cot_h)
    near = (ws, seeds, wn, means, cot)
    loads = [pltpu.make_async_copy(given[i], near[i], sems.at[i]) for i in range(5)]
    for load in loads:
        load.start()
    nf, rows, _ = grad.shape
    cols = rows // 2
    for load in loads[:2]:
        load.wait()
    total = jnp.dot(ws[...], seeds[...], preferred_element_type=F32)
    for load in loads[2:4]:
        load.wait()
    total += jnp.dot(wn[...], means[...], preferred_element_type=F32)
    h = jnp.maximum(total, 0.0).astype(BF16)
    hid[...] = h
    stores = [pltpu.make_async_copy(hid, hid_h, sems.at[5])]
    stores[0].start()
    loads[4].wait()
    dpre = jnp.where(h > 0, cot[...], jnp.zeros_like(h))
    dims = (((1,), (1,)), ((), ()))
    for j, x in enumerate((seeds, means)):
        at = j * cols
        g = lax.dot_general(x[...], dpre, dims, preferred_element_type=F32).astype(BF16)
        for i in range(nf):
            grad[i, at : at + cols, :] = g[i * cols : (i + 1) * cols]
        where = (slice(None), pl.ds(at, cols), slice(None))
        store = pltpu.make_async_copy(grad.at[where], grad_h.at[where], sems.at[6 + j])
        store.start()
        stores.append(store)
    for store in stores:
        store.wait()


def layer(ws_t, seeds, wn_t, means, cot, nf):
    hcols, rows = cot.shape
    args = (ws_t, seeds, wn_t, means, cot)
    shapes = [(hcols, rows), (nf, 2 * means.shape[0] // nf, hcols)]
    return pl.pallas_call(
        layer_kernel,
        in_specs=[HBM] * 5,
        out_specs=[HBM] * 2,
        out_shape=[pltpu.HBM(o, BF16) for o in shapes],
        scratch_shapes=[pltpu.VMEM(a.shape, a.dtype) for a in args]
        + [pltpu.VMEM(o, BF16) for o in shapes]
        + [pltpu.SemaphoreType.DMA((8,))],
        compiler_params=pltpu.CompilerParams(vmem_limit_bytes=40 * 1024 * 1024),
    )(*far(*args))


def shards(seed_feats, src_feats, counts, dst_block, src_block, w_self, w_neigh, cotangent):
    seeds_here, cols = seed_feats.shape
    ng = lax.axis_size("group")
    nf = lax.axis_size("feat")
    part = seeds_here // SIDE
    ccols = cotangent.shape[1]
    hcols = SIDE * ccols
    f = lax.axis_index("feat")
    fx, fy = f // SIDE, f % SIDE
    along_y = [[x * SIDE + y for y in range(SIDE)] for x in range(SIDE)]

    def shift_y(a, k):
        return lax.ppermute(
            a, "feat", [(i, i // SIDE * SIDE + (i % SIDE + k) % SIDE) for i in range(nf)]
        )

    with jax.named_scope("tile_sums"):
        sums, deg = tile_sums(dst_block, src_block, src_feats.T, counts, ng, seeds_here)

    with jax.named_scope("neighbour_sum"):
        total = lax.psum_scatter(
            sums.reshape(ng * cols, seeds_here), "group", scatter_dimension=0, tiled=True
        )

    seed_t, cot_t, deg, _ = lax.optimization_barrier((seed_feats.T, cotangent.T, deg, sums))

    with jax.named_scope("degree"):
        degree = jnp.sum(lax.all_to_all(deg[:, 0], "group", 0, 0, tiled=True), axis=0)[None]

    with jax.named_scope("cotangent_rows"):
        send = cot_t.reshape(ccols, SIDE, part).transpose(1, 0, 2)
        cot = lax.all_to_all(send, "feat", 0, 0, axis_index_groups=along_y)
        cot = cot.reshape(hcols, part)

    with jax.named_scope("seed_rows"):
        send = seed_t.reshape(cols, SIDE, part).transpose(1, 0, 2)
        send = jnp.broadcast_to(send[None], (SIDE, SIDE, cols, part)).reshape(nf, cols, part)
        seeds = lax.all_to_all(send, "feat", 0, 0).reshape(nf * cols, part)

    with jax.named_scope("weights"):
        ws_t = lax.dynamic_slice_in_dim(w_self, fx * hcols, hcols, 1).T
        wn_t = lax.dynamic_slice_in_dim(w_neigh, fx * hcols, hcols, 1).T

    with jax.named_scope("mean_rows"):
        total, degree, seeds, cot, ws_t, wn_t = lax.optimization_barrier(
            (total, degree, seeds, cot, ws_t, wn_t)
        )
        send = mean_rows(total, degree)
        means = lax.all_to_all(send, "feat", 0, 0).reshape(nf * cols, part)

    with jax.named_scope("layer"):
        hid, both = layer(ws_t, seeds, wn_t, means, cot, nf)

    with jax.named_scope("grads"):
        got = lax.all_to_all(both, "feat", 0, 0).astype(F32)
        got = jnp.sum(got.reshape(SIDE, SIDE, 2 * cols, hcols), axis=1)
        got = got.reshape(SIDE, 2 * cols, 2, hcols // 2).transpose(0, 2, 1, 3)
        got = got.reshape(ng, 2 * cols, hcols // 2).astype(BF16)
        got, hid = lax.optimization_barrier((got, hid))
        got = jnp.sum(lax.all_to_all(got, "group", 0, 0).astype(F32), axis=0)

    with jax.named_scope("hidden_columns"):
        hid4 = hid.reshape(SIDE, ccols, part)
        pieces = []
        for k in range(SIDE):
            piece = lax.dynamic_index_in_dim(hid4, (fy + k) % SIDE, 0, keepdims=False)
            pieces.append(shift_y(piece, k) if k else piece)
        got, *pieces = lax.optimization_barrier((got, *pieces))
        out = jnp.zeros((ccols, seeds_here), BF16)
        for k in range(SIDE):
            out = lax.dynamic_update_slice(out, pieces[k], (0, (fy - k) % SIDE * part))
    return (out.T, got[:cols], got[cols:])


def solution(mesh):
    in_specs = (
        P(("rep", "group"), "feat"),
        P(("rep", "group"), "feat"),
        P(("rep", "group"), None, None),
        P(("rep", "group")),
        P(("rep", "group")),
        P(),
        P(),
        P(("rep", "group"), "feat"),
    )
    out_specs = (
        P(("rep", "group"), "feat"),
        P(("rep", "feat"), "group"),
        P(("rep", "feat"), "group"),
    )
    return jax.shard_map(shards, mesh=mesh, in_specs=in_specs, out_specs=out_specs, check_vma=False)
```

```python
import jax
import jax.numpy as jnp
from jax import lax
from jax.experimental import pallas as pl
from jax.experimental.pallas import tpu as pltpu
from jax.sharding import PartitionSpec as P

F32, BF16 = jnp.float32, jnp.bfloat16
UNROLL = 16
SIDE = 4
EARLY = 7
HBM = pl.BlockSpec(memory_space=pltpu.HBM)


def far(*arrays):
    return [pltpu.with_memory_space_constraint(a, pltpu.HBM) for a in arrays]


def tile_kernel(me, dst_h, src_h, feats_h, counts_h, sums_h, *refs):
    *late_h, deg_h, dst, src, feats, counts, acc, deg, held, short, sems = refs
    per_part = acc.shape[2] // held.shape[2] // SIDE
    early = sums_h.shape[2]
    cols = feats.shape[0]
    nsrc, rows, tile = held.shape
    owners, _, seeds_here = acc.shape
    per_owner = seeds_here // tile
    ntile = counts.shape[0]
    nload = ntile // UNROLL

    def load_counts(c):
        where = pl.ds(c * UNROLL, UNROLL)
        return pltpu.make_async_copy(counts_h.at[where], counts.at[where], sems.at[c])

    loads = [
        pltpu.make_async_copy(dst_h, dst, sems.at[nload]),
        pltpu.make_async_copy(src_h, src, sems.at[nload + 1]),
        pltpu.make_async_copy(feats_h, feats, sems.at[nload + 2]),
    ]
    for load in loads:
        load.start()
    for c in range(nload):
        load_counts(c).start()
    acc[...] = jnp.zeros_like(acc)
    deg[...] = jnp.zeros_like(deg)
    held[:, cols:, :] = jnp.ones((nsrc, rows - cols, tile), BF16)
    for load in loads:
        load.wait()
    for b in range(nsrc):
        held[b, :cols, :] = feats[:, b * tile : (b + 1) * tile]

    def chunk(c, _):
        load_counts(c).wait()
        for u in range(UNROLL):
            t = c * UNROLL + u
            d = dst[t]
            got = lax.dot_general(
                held[src[t]],
                counts[t].astype(F32).astype(BF16),
                (((1,), (1,)), ((), ())),
                preferred_element_type=F32,
            )
            owner, blk = d // per_owner, d % per_owner
            y, r = blk // per_part, blk % per_part
            late_at = SIDE * EARLY + y * (per_part - EARLY) + r - EARLY
            at = jnp.where(r < EARLY, y * EARLY + r, late_at)
            lanes = pl.ds(pl.multiple_of(at * tile, tile), tile)
            acc[owner, :, lanes] += got[:cols]
            deg[owner, :, lanes] += got[cols : cols + 8]
        return _

    lax.fori_loop(0, nload, chunk, 0)
    stores = []
    for k in (4, 5):
        stores.append((acc.at[lax.rem(me[0] + k, owners), :, pl.ds(early, seeds_here - early)], late_h[k]))
    width = short.shape[2]
    for o in range(owners):
        for r in range(short.shape[1]):
            short[o, r : r + 1, :] = deg[o, :1, r * width : (r + 1) * width]
    stores.append((short, deg_h))
    stores.append((acc.at[:, :, pl.ds(0, early)], sums_h))
    for k in (3, 6, 2, 7, 1, 0):
        stores.append((acc.at[lax.rem(me[0] + k, owners), :, pl.ds(early, seeds_here - early)], late_h[k]))
    stores = [pltpu.make_async_copy(p, q, sems.at[i]) for i, (p, q) in enumerate(stores)]
    for store in stores:
        store.start()
    for store in stores:
        store.wait()


def tile_sums(me, dst_block, src_block, feats_t, counts, owners, seeds_here):
    ntile, tile, _ = counts.shape
    cols, sources = feats_t.shape
    early = seeds_here // 8 * EARLY
    outs = [(owners, cols, early)] + [(cols, seeds_here - early)] * owners
    outs.append((owners, 8, seeds_here // 8))
    sums, *late, deg = pl.pallas_call(
        tile_kernel,
        in_specs=[pl.BlockSpec(memory_space=pltpu.SMEM)] + [HBM] * 4,
        out_specs=[HBM] * len(outs),
        out_shape=[pltpu.HBM(o, F32) for o in outs],
        scratch_shapes=[
            pltpu.SMEM((ntile,), jnp.int32),
            pltpu.SMEM((ntile,), jnp.int32),
            pltpu.VMEM((cols, sources), BF16),
            pltpu.VMEM(counts.shape, jnp.int32),
            pltpu.VMEM((owners, cols, seeds_here), F32),
            pltpu.VMEM((owners, 8, seeds_here), F32),
            pltpu.VMEM((sources // tile, cols + 16, tile), BF16),
            pltpu.VMEM((owners, 8, seeds_here // 8), F32),
            pltpu.SemaphoreType.DMA((max(ntile // UNROLL + 3, len(outs)),)),
        ],
        compiler_params=pltpu.CompilerParams(vmem_limit_bytes=40 * 1024 * 1024),
    )(me, *far(dst_block, src_block, feats_t, counts))
    return sums, late, deg


def mean_kernel(total_h, degree_h, send_h, total, degree, send, sems):
    width = send.shape[2]
    lanes = [pl.ds(y * width, width) for y in range(SIDE)]
    first = pltpu.make_async_copy(degree_h, degree, sems.at[0])
    first.start()
    loads = [
        pltpu.make_async_copy(total_h.at[:, lanes[y]], total.at[:, lanes[y]], sems.at[1 + y])
        for y in range(SIDE)
    ]
    for load in loads:
        load.start()
    first.wait()
    stores = []
    for y in range(SIDE):
        loads[y].wait()
        send[y] = (total[:, lanes[y]] / (degree[:, lanes[y]] + 1.0)).astype(BF16)
        for x in range(SIDE):
            i = x * SIDE + y
            store = pltpu.make_async_copy(send.at[y], send_h.at[i], sems.at[1 + SIDE + i])
            store.start()
            stores.append(store)
    for store in stores:
        store.wait()


def mean_rows(total, degree):
    cols, n = total.shape
    send = (SIDE, cols, n // SIDE)
    return pl.pallas_call(
        mean_kernel,
        in_specs=[HBM, HBM],
        out_specs=HBM,
        out_shape=pltpu.HBM((SIDE * SIDE, *send[1:]), BF16),
        scratch_shapes=[
            pltpu.VMEM(total.shape, F32),
            pltpu.VMEM(degree.shape, F32),
            pltpu.VMEM(send, BF16),
            pltpu.SemaphoreType.DMA((1 + SIDE + SIDE * SIDE,)),
        ],
        compiler_params=pltpu.CompilerParams(vmem_limit_bytes=16 * 1024 * 1024),
    )(*far(total), degree)


def layer_kernel(lo, last, *refs):
    nin = 7 if last else 5
    given, (hid_h, grad_h) = refs[:nin], refs[nin : nin + 2]
    ws, seeds, wn, means, cot, hid, grad, *rest = refs[nin + 2 :]
    sems = rest[-1]
    width = means.shape[1]
    lanes = (slice(None), pl.ds(lo, width))
    pairs = [
        (given[0], ws),
        (given[1].at[lanes], seeds),
        (given[2], wn),
        (given[3], means),
        (given[4].at[lanes], cot),
    ]
    if last:
        pairs.append((given[6], rest[0]))
    loads = [pltpu.make_async_copy(p, q, sems.at[i]) for i, (p, q) in enumerate(pairs)]
    for load in loads:
        load.start()
    for load in loads[:2]:
        load.wait()
    total = jnp.dot(ws[...], seeds[...], preferred_element_type=F32)
    for load in loads[2:4]:
        load.wait()
    total += jnp.dot(wn[...], means[...], preferred_element_type=F32)
    h = jnp.maximum(total, 0.0).astype(BF16)
    hid[...] = h
    stores = [pltpu.make_async_copy(hid, hid_h.at[lanes], sems.at[6])]
    stores[0].start()
    for load in loads[4:]:
        load.wait()
    dpre = jnp.where(h > 0, cot[...], jnp.zeros_like(h))
    dims = (((1,), (1,)), ((), ()))
    for j, x in enumerate((seeds, means)):
        g = lax.dot_general(x[...], dpre, dims, preferred_element_type=F32)
        if last:
            g = (g + rest[0][j]).astype(BF16)
            cols = grad.shape[1] // 2
            at = j * cols
            for i in range(grad.shape[0]):
                grad[i, at : at + cols, :] = g[i * cols : (i + 1) * cols]
            where = (slice(None), pl.ds(at, cols), slice(None))
        else:
            grad[j] = g
            where = j
        store = pltpu.make_async_copy(grad.at[where], grad_h.at[where], sems.at[7 + j])
        store.start()
        stores.append(store)
    for store in stores:
        store.wait()


def layer(ws_t, seeds, wn_t, means, cot, lo, before, nf):
    hcols, rows = cot.shape
    depth, width = means.shape
    last = before is not None
    args = (ws_t, seeds, wn_t, means, cot) + (before if last else ())
    grad = ((nf, 2 * depth // nf, hcols), BF16) if last else ((2, depth, hcols), F32)
    near = [
        ((hcols, depth), BF16),
        ((depth, width), BF16),
        ((hcols, depth), BF16),
        ((depth, width), BF16),
        ((hcols, width), BF16),
        ((hcols, width), BF16),
        grad,
    ]
    if last:
        near.append(((2, depth, hcols), F32))
    return pl.pallas_call(
        lambda *refs: layer_kernel(lo, last, *refs),
        in_specs=[HBM] * len(args),
        out_specs=[HBM] * 2,
        out_shape=[pltpu.HBM((hcols, rows), BF16), pltpu.HBM(*grad)],
        scratch_shapes=[pltpu.VMEM(*n) for n in near] + [pltpu.SemaphoreType.DMA((9,))],
        input_output_aliases={5: 0} if last else {},
        compiler_params=pltpu.CompilerParams(vmem_limit_bytes=40 * 1024 * 1024),
    )(*far(*args))


def shards(seed_feats, src_feats, counts, dst_block, src_block, w_self, w_neigh, cotangent):
    seeds_here, cols = seed_feats.shape
    ng = lax.axis_size("group")
    nf = lax.axis_size("feat")
    part = seeds_here // SIDE
    ccols = cotangent.shape[1]
    hcols = SIDE * ccols
    f = lax.axis_index("feat")
    fx, fy = f // SIDE, f % SIDE
    along_y = [[x * SIDE + y for y in range(SIDE)] for x in range(SIDE)]

    def shift_y(a, k):
        return lax.ppermute(
            a, "feat", [(i, i // SIDE * SIDE + (i % SIDE + k) % SIDE) for i in range(nf)]
        )

    def shift_z(a, k):
        return lax.ppermute(a, "group", [(i, (i + k) % ng) for i in range(ng)])

    def meet(*arrays):
        return lax.optimization_barrier(arrays)

    with jax.named_scope("tile_sums"):
        me = lax.axis_index("group")[None].astype(jnp.int32)
        sums, late, deg = tile_sums(
            me, dst_block, src_block, src_feats.T, counts, ng, seeds_here
        )

    with jax.named_scope("neighbour_sum"):
        total = lax.psum_scatter(
            sums.reshape(ng * cols, -1), "group", scatter_dimension=0, tiled=True
        )

    with jax.named_scope("weights"):
        ws_t = lax.dynamic_slice_in_dim(w_self, fx * hcols, hcols, 1).T
        wn_t = lax.dynamic_slice_in_dim(w_neigh, fx * hcols, hcols, 1).T

    with jax.named_scope("hop_1"):
        up = shift_z(late[4], 1)
        down = shift_z(late[5], -1)
        up, down, seed_t = meet(up, down, seed_feats.T)

    with jax.named_scope("degree"):
        degree = jnp.sum(lax.all_to_all(deg, "group", 0, 0), axis=0).reshape(1, seeds_here)

    with jax.named_scope("seed_rows"):
        send = seed_t.reshape(cols, SIDE, part).transpose(1, 0, 2)
        send = jnp.broadcast_to(send[None], (SIDE, SIDE, cols, part)).reshape(nf, cols, part)
        seeds = lax.all_to_all(send, "feat", 0, 0).reshape(nf * cols, part)

    with jax.named_scope("hop_2"):
        up = shift_z(up + late[3], 1)
        down = shift_z(down + late[6], -1)
        up, down, degree, cot_t = meet(up, down, degree, cotangent.T)

    with jax.named_scope("cotangent_rows"):
        send = cot_t.reshape(ccols, SIDE, part).transpose(1, 0, 2)
        cot = lax.all_to_all(send, "feat", 0, 0, axis_index_groups=along_y)
        cot = cot.reshape(hcols, part)

    with jax.named_scope("hop_3"):
        up = shift_z(up + late[2], 1)
        down = shift_z(down + late[7], -1)
        up, down, seeds = meet(up, down, seeds)

    with jax.named_scope("hop_4"):
        up = shift_z(up + late[1], 1)
        total2, cot = meet(late[0] + up + down, cot)

    early = total.shape[1]
    before = None
    for x, lo, hi in ((total2, early, seeds_here), (total, 0, early)):
        with jax.named_scope("mean_rows_%d" % lo):
            send = mean_rows(x, degree[:, lo:hi])
            means = lax.all_to_all(send, "feat", 0, 0).reshape(nf * cols, -1)
        with jax.named_scope("layer_%d" % lo):
            before = layer(ws_t, seeds, wn_t, means, cot, lo // SIDE, before, nf)
    hid, both = before

    with jax.named_scope("grads"):
        got = lax.all_to_all(both, "feat", 0, 0).astype(F32)
        got = jnp.sum(got.reshape(SIDE, SIDE, 2 * cols, hcols), axis=1)
        got = got.reshape(SIDE, 2 * cols, 2, hcols // 2).transpose(0, 2, 1, 3)
        got = got.reshape(ng, 2 * cols, hcols // 2).astype(BF16)
        got, hid = lax.optimization_barrier((got, hid))
        got = jnp.sum(lax.all_to_all(got, "group", 0, 0).astype(F32), axis=0)

    with jax.named_scope("hidden_columns"):
        hid4 = hid.reshape(SIDE, ccols, part)
        pieces = []
        for k in range(SIDE):
            piece = lax.dynamic_index_in_dim(hid4, (fy + k) % SIDE, 0, keepdims=False)
            pieces.append(shift_y(piece, k) if k else piece)
        got, *pieces = lax.optimization_barrier((got, *pieces))
        out = jnp.zeros((ccols, seeds_here), BF16)
        for k in range(SIDE):
            out = lax.dynamic_update_slice(out, pieces[k], (0, (fy - k) % SIDE * part))
    return (out.T, got[:cols], got[cols:])


def solution(mesh):
    in_specs = (
        P(("rep", "group"), "feat"),
        P(("rep", "group"), "feat"),
        P(("rep", "group"), None, None),
        P(("rep", "group")),
        P(("rep", "group")),
        P(),
        P(),
        P(("rep", "group"), "feat"),
    )
    out_specs = (
        P(("rep", "group"), "feat"),
        P(("rep", "feat"), "group"),
        P(("rep", "feat"), "group"),
    )
    return jax.shard_map(shards, mesh=mesh, in_specs=in_specs, out_specs=out_specs, check_vma=False)
```

```python
import jax
import jax.numpy as jnp
from jax import lax
from jax.experimental import pallas as pl
from jax.experimental.pallas import tpu as pltpu
from jax.sharding import PartitionSpec as P

F32, BF16 = jnp.float32, jnp.bfloat16
UNROLL = 16
SIDE = 4
EARLY = 7
HBM = pl.BlockSpec(memory_space=pltpu.HBM)


def far(*arrays):
    return [pltpu.with_memory_space_constraint(a, pltpu.HBM) for a in arrays]


def tile_kernel(me, dst_h, src_h, feats_h, counts_h, sums_h, *refs):
    *late_h, deg_h, dst, src, feats, counts, acc, deg, held, short, sems = refs
    per_part = acc.shape[2] // held.shape[2] // SIDE
    early = sums_h.shape[2]
    cols = feats.shape[0]
    nsrc, rows, tile = held.shape
    owners, _, seeds_here = acc.shape
    per_owner = seeds_here // tile
    ntile = counts.shape[0]
    nload = ntile // UNROLL

    def load_counts(c):
        where = pl.ds(c * UNROLL, UNROLL)
        return pltpu.make_async_copy(counts_h.at[where], counts.at[where], sems.at[c])

    loads = [
        pltpu.make_async_copy(dst_h, dst, sems.at[nload]),
        pltpu.make_async_copy(src_h, src, sems.at[nload + 1]),
        pltpu.make_async_copy(feats_h, feats, sems.at[nload + 2]),
    ]
    for load in loads:
        load.start()
    for c in range(nload):
        load_counts(c).start()
    acc[...] = jnp.zeros_like(acc)
    deg[...] = jnp.zeros_like(deg)
    held[:, cols:, :] = jnp.ones((nsrc, rows - cols, tile), BF16)
    for load in loads:
        load.wait()
    for b in range(nsrc):
        held[b, :cols, :] = feats[:, b * tile : (b + 1) * tile]

    def chunk(c, _):
        load_counts(c).wait()
        for u in range(UNROLL):
            t = c * UNROLL + u
            d = dst[t]
            got = lax.dot_general(
                held[src[t]],
                counts[t].astype(F32).astype(BF16),
                (((1,), (1,)), ((), ())),
                preferred_element_type=F32,
            )
            owner, blk = d // per_owner, d % per_owner
            y, r = blk // per_part, blk % per_part
            late_at = SIDE * EARLY + y * (per_part - EARLY) + r - EARLY
            at = jnp.where(r < EARLY, y * EARLY + r, late_at)
            lanes = pl.ds(pl.multiple_of(at * tile, tile), tile)
            acc[owner, :, lanes] += got[:cols]
            deg[owner, :, lanes] += got[cols : cols + 8]
        return _

    lax.fori_loop(0, nload, chunk, 0)
    stores = []
    for k in (4, 5):
        stores.append((acc.at[lax.rem(me[0] + k, owners), :, pl.ds(early, seeds_here - early)], late_h[k]))
    width = short.shape[2]
    for o in range(owners):
        for r in range(short.shape[1]):
            short[o, r : r + 1, :] = deg[o, :1, r * width : (r + 1) * width]
    stores.append((short, deg_h))
    stores.append((acc.at[:, :, pl.ds(0, early)], sums_h))
    for k in (3, 6, 2, 7, 1, 0):
        stores.append((acc.at[lax.rem(me[0] + k, owners), :, pl.ds(early, seeds_here - early)], late_h[k]))
    stores = [pltpu.make_async_copy(p, q, sems.at[i]) for i, (p, q) in enumerate(stores)]
    for store in stores:
        store.start()
    for store in stores:
        store.wait()


def tile_sums(me, dst_block, src_block, feats_t, counts, owners, seeds_here):
    ntile, tile, _ = counts.shape
    cols, sources = feats_t.shape
    early = seeds_here // 8 * EARLY
    outs = [(owners, cols, early)] + [(cols, seeds_here - early)] * owners
    outs.append((owners, 8, seeds_here // 8))
    sums, *late, deg = pl.pallas_call(
        tile_kernel,
        in_specs=[pl.BlockSpec(memory_space=pltpu.SMEM)] + [HBM] * 4,
        out_specs=[HBM] * len(outs),
        out_shape=[pltpu.HBM(o, F32) for o in outs],
        scratch_shapes=[
            pltpu.SMEM((ntile,), jnp.int32),
            pltpu.SMEM((ntile,), jnp.int32),
            pltpu.VMEM((cols, sources), BF16),
            pltpu.VMEM(counts.shape, jnp.int32),
            pltpu.VMEM((owners, cols, seeds_here), F32),
            pltpu.VMEM((owners, 8, seeds_here), F32),
            pltpu.VMEM((sources // tile, cols + 16, tile), BF16),
            pltpu.VMEM((owners, 8, seeds_here // 8), F32),
            pltpu.SemaphoreType.DMA((max(ntile // UNROLL + 3, len(outs)),)),
        ],
        compiler_params=pltpu.CompilerParams(vmem_limit_bytes=40 * 1024 * 1024),
    )(me, *far(dst_block, src_block, feats_t, counts))
    return sums, late, deg


def mean_kernel(total_h, degree_h, send_h, total, degree, send, sems):
    width = send.shape[2]
    lanes = [pl.ds(y * width, width) for y in range(SIDE)]
    first = pltpu.make_async_copy(degree_h, degree, sems.at[0])
    first.start()
    loads = [
        pltpu.make_async_copy(total_h.at[:, lanes[y]], total.at[:, lanes[y]], sems.at[1 + y])
        for y in range(SIDE)
    ]
    for load in loads:
        load.start()
    first.wait()
    stores = []
    for y in range(SIDE):
        loads[y].wait()
        send[y] = (total[:, lanes[y]] / (degree[:, lanes[y]] + 1.0)).astype(BF16)
        for x in range(SIDE):
            i = x * SIDE + y
            store = pltpu.make_async_copy(send.at[y], send_h.at[i], sems.at[1 + SIDE + i])
            store.start()
            stores.append(store)
    for store in stores:
        store.wait()


def mean_rows(total, degree):
    cols, n = total.shape
    send = (SIDE, cols, n // SIDE)
    return pl.pallas_call(
        mean_kernel,
        in_specs=[HBM, HBM],
        out_specs=HBM,
        out_shape=pltpu.HBM((SIDE * SIDE, *send[1:]), BF16),
        scratch_shapes=[
            pltpu.VMEM(total.shape, F32),
            pltpu.VMEM(degree.shape, F32),
            pltpu.VMEM(send, BF16),
            pltpu.SemaphoreType.DMA((1 + SIDE + SIDE * SIDE,)),
        ],
        compiler_params=pltpu.CompilerParams(vmem_limit_bytes=16 * 1024 * 1024),
    )(*far(total), degree)


def late_kernel(ws_h, seeds_h, wn_h, means_h, hid_h, pre_h, ws, seeds, wn, means, hid, pre, sems):
    early = pre.shape[1]
    pairs = ((ws_h, ws), (seeds_h, seeds), (wn_h, wn), (means_h, means))
    loads = [pltpu.make_async_copy(p, q, sems.at[i]) for i, (p, q) in enumerate(pairs)]
    for load in loads:
        load.start()
    for load in loads:
        load.wait()
    total = jnp.dot(ws[...], seeds[...], preferred_element_type=F32)
    pre[...] = total[:, :early]
    total = total[:, early:] + jnp.dot(wn[...], means[...], preferred_element_type=F32)
    hid[...] = jnp.maximum(total, 0.0).astype(BF16)
    lanes = (slice(None), pl.ds(early, hid.shape[1]))
    stores = [
        pltpu.make_async_copy(hid, hid_h.at[lanes], sems.at[4]),
        pltpu.make_async_copy(pre, pre_h, sems.at[5]),
    ]
    for store in stores:
        store.start()
    for store in stores:
        store.wait()


def late_rows(ws_t, seeds, wn_t, means):
    hcols, _ = ws_t.shape
    rows, late = seeds.shape[1], means.shape[1]
    return pl.pallas_call(
        late_kernel,
        in_specs=[HBM] * 3 + [pl.BlockSpec(memory_space=pl.ANY)],
        out_specs=[HBM] * 2,
        out_shape=[pltpu.HBM((hcols, rows), BF16), pltpu.HBM((hcols, rows - late), F32)],
        scratch_shapes=[pltpu.VMEM(a.shape, BF16) for a in (ws_t, seeds, wn_t, means)]
        + [
            pltpu.VMEM((hcols, late), BF16),
            pltpu.VMEM((hcols, rows - late), F32),
            pltpu.SemaphoreType.DMA((6,)),
        ],
        compiler_params=pltpu.CompilerParams(vmem_limit_bytes=32 * 1024 * 1024),
    )(*far(ws_t, seeds, wn_t), means)


def layer_kernel(wn_h, means_h, pre_h, cot_h, late_h, before_h, seeds_h, hid_h, grad_h, *refs):
    wn, means, pre, cot, seeds, hid, grad, sems = refs
    early, rows = pre.shape[1], cot.shape[1]
    first = (slice(None), pl.ds(0, early))
    rest = (slice(None), pl.ds(early, rows - early))
    pairs = (
        (wn_h, wn),
        (means_h, means.at[first]),
        (pre_h, pre),
        (cot_h, cot),
        (before_h.at[rest], hid.at[rest]),
        (seeds_h, seeds),
        (late_h, means.at[rest]),
    )
    loads = [pltpu.make_async_copy(p, q, sems.at[i]) for i, (p, q) in enumerate(pairs)]
    for load in loads:
        load.start()
    for load in loads[:3]:
        load.wait()
    total = pre[...] + jnp.dot(wn[...], means[first], preferred_element_type=F32)
    hid[first] = jnp.maximum(total, 0.0).astype(BF16)
    stores = [pltpu.make_async_copy(hid.at[first], hid_h.at[first], sems.at[7])]
    stores[0].start()
    for load in loads[3:]:
        load.wait()
    dpre = jnp.where(hid[...] > 0, cot[...], jnp.zeros_like(cot))
    dims = (((1,), (1,)), ((), ()))
    nf, cols = grad.shape[0], grad.shape[1] // 2
    for j, x in enumerate((seeds, means)):
        at = j * cols
        g = lax.dot_general(x[...], dpre, dims, preferred_element_type=F32).astype(BF16)
        for i in range(nf):
            grad[i, at : at + cols, :] = g[i * cols : (i + 1) * cols]
        where = (slice(None), pl.ds(at, cols), slice(None))
        store = pltpu.make_async_copy(grad.at[where], grad_h.at[where], sems.at[8 + j])
        store.start()
        stores.append(store)
    for store in stores:
        store.wait()


def layer(wn_t, means, pre, cot, late, before, seeds, nf):
    hcols, rows = cot.shape
    depth, early = means.shape
    grad = (nf, 2 * depth // nf, hcols)
    anywhere = pl.BlockSpec(memory_space=pl.ANY)
    return pl.pallas_call(
        layer_kernel,
        in_specs=[HBM, anywhere] + [HBM] * 2 + [anywhere] + [HBM] * 2,
        out_specs=[HBM] * 2,
        out_shape=[pltpu.HBM((hcols, rows), BF16), pltpu.HBM(grad, BF16)],
        scratch_shapes=[
            pltpu.VMEM((hcols, depth), BF16),
            pltpu.VMEM((depth, rows), BF16),
            pltpu.VMEM((hcols, early), F32),
            pltpu.VMEM((hcols, rows), BF16),
            pltpu.VMEM((depth, rows), BF16),
            pltpu.VMEM((hcols, rows), BF16),
            pltpu.VMEM(grad, BF16),
            pltpu.SemaphoreType.DMA((10,)),
        ],
        input_output_aliases={5: 0},
        compiler_params=pltpu.CompilerParams(vmem_limit_bytes=40 * 1024 * 1024),
    )(*far(wn_t), means, *far(pre, cot), late, *far(before, seeds))


def shards(seed_feats, src_feats, counts, dst_block, src_block, w_self, w_neigh, cotangent):
    seeds_here, cols = seed_feats.shape
    ng = lax.axis_size("group")
    nf = lax.axis_size("feat")
    part = seeds_here // SIDE
    ccols = cotangent.shape[1]
    hcols = SIDE * ccols
    f = lax.axis_index("feat")
    fx, fy = f // SIDE, f % SIDE
    along_y = [[x * SIDE + y for y in range(SIDE)] for x in range(SIDE)]

    def shift_y(a, k):
        return lax.ppermute(
            a, "feat", [(i, i // SIDE * SIDE + (i % SIDE + k) % SIDE) for i in range(nf)]
        )

    def shift_z(a, k):
        return lax.ppermute(a, "group", [(i, (i + k) % ng) for i in range(ng)])

    def meet(*arrays):
        return lax.optimization_barrier(arrays)

    with jax.named_scope("tile_sums"):
        me = lax.axis_index("group")[None].astype(jnp.int32)
        sums, late, deg = tile_sums(
            me, dst_block, src_block, src_feats.T, counts, ng, seeds_here
        )

    with jax.named_scope("neighbour_sum"):
        total = lax.psum_scatter(
            sums.reshape(ng * cols, -1), "group", scatter_dimension=0, tiled=True
        )

    with jax.named_scope("weights"):
        ws_t = lax.dynamic_slice_in_dim(w_self, fx * hcols, hcols, 1).T
        wn_t = lax.dynamic_slice_in_dim(w_neigh, fx * hcols, hcols, 1).T

    with jax.named_scope("hop_1"):
        up = shift_z(late[4], 1)
        down = shift_z(late[5], -1)
        up, down, seed_t = meet(up, down, seed_feats.T)

    with jax.named_scope("degree"):
        degree = jnp.sum(lax.all_to_all(deg, "group", 0, 0), axis=0).reshape(1, seeds_here)

    with jax.named_scope("seed_rows"):
        send = seed_t.reshape(cols, SIDE, part).transpose(1, 0, 2)
        send = jnp.broadcast_to(send[None], (SIDE, SIDE, cols, part)).reshape(nf, cols, part)
        seeds = lax.all_to_all(send, "feat", 0, 0).reshape(nf * cols, part)

    with jax.named_scope("hop_2"):
        up = shift_z(up + late[3], 1)
        down = shift_z(down + late[6], -1)
        up, down, degree, cot_t = meet(up, down, degree, cotangent.T)

    with jax.named_scope("cotangent_rows"):
        send = cot_t.reshape(ccols, SIDE, part).transpose(1, 0, 2)
        cot = lax.all_to_all(send, "feat", 0, 0, axis_index_groups=along_y)
        cot = cot.reshape(hcols, part)

    with jax.named_scope("hop_3"):
        up = shift_z(up + late[2], 1)
        down = shift_z(down + late[7], -1)
        up, down, seeds = meet(up, down, seeds)

    with jax.named_scope("hop_4"):
        up = shift_z(up + late[1], 1)
        total2, cot = meet(late[0] + up + down, cot)

    early = total.shape[1]
    means = []
    for x, lo, hi in ((total2, early, seeds_here), (total, 0, early)):
        with jax.named_scope("mean_rows_%d" % lo):
            send = mean_rows(x, degree[:, lo:hi])
            means.append(lax.all_to_all(send, "feat", 0, 0).reshape(nf * cols, -1))

    with jax.named_scope("layer"):
        hid, pre = late_rows(ws_t, seeds, wn_t, means[0])
        hid, both = layer(wn_t, means[1], pre, cot, means[0], hid, seeds, nf)

    with jax.named_scope("grads"):
        got = lax.all_to_all(both, "feat", 0, 0).astype(F32)
        got = jnp.sum(got.reshape(SIDE, SIDE, 2 * cols, hcols), axis=1)
        got = got.reshape(SIDE, 2 * cols, 2, hcols // 2).transpose(0, 2, 1, 3)
        got = got.reshape(ng, 2 * cols, hcols // 2).astype(BF16)
        got, hid = lax.optimization_barrier((got, hid))
        got = jnp.sum(lax.all_to_all(got, "group", 0, 0).astype(F32), axis=0)

    with jax.named_scope("hidden_columns"):
        hid4 = hid.reshape(SIDE, ccols, part)
        pieces = []
        for k in range(SIDE):
            piece = lax.dynamic_index_in_dim(hid4, (fy + k) % SIDE, 0, keepdims=False)
            pieces.append(shift_y(piece, k) if k else piece)
        got, *pieces = lax.optimization_barrier((got, *pieces))
        out = jnp.zeros((ccols, seeds_here), BF16)
        for k in range(SIDE):
            out = lax.dynamic_update_slice(out, pieces[k], (0, (fy - k) % SIDE * part))
    return (out.T, got[:cols], got[cols:])


def solution(mesh):
    in_specs = (
        P(("rep", "group"), "feat"),
        P(("rep", "group"), "feat"),
        P(("rep", "group"), None, None),
        P(("rep", "group")),
        P(("rep", "group")),
        P(),
        P(),
        P(("rep", "group"), "feat"),
    )
    out_specs = (
        P(("rep", "group"), "feat"),
        P(("rep", "feat"), "group"),
        P(("rep", "feat"), "group"),
    )
    return jax.shard_map(shards, mesh=mesh, in_specs=in_specs, out_specs=out_specs, check_vma=False)
```

```python
import jax
import jax.numpy as jnp
from jax import lax
from jax.experimental import pallas as pl
from jax.experimental.pallas import tpu as pltpu
from jax.sharding import PartitionSpec as P

F32, BF16 = jnp.float32, jnp.bfloat16
UNROLL = 16
SIDE = 4
EARLY = 6
HBM = pl.BlockSpec(memory_space=pltpu.HBM)


def far(*arrays):
    return [pltpu.with_memory_space_constraint(a, pltpu.HBM) for a in arrays]


def tile_kernel(me, dst_h, src_h, feats_h, counts_h, sums_h, *refs):
    *late_h, deg_h, dst, src, feats, counts, acc, deg, held, short, far_sums, sems = refs
    per_part = acc.shape[2] // held.shape[2] // SIDE
    early = sums_h.shape[2]
    cols = feats.shape[0]
    nsrc, rows, tile = held.shape
    owners, _, seeds_here = acc.shape
    per_owner = seeds_here // tile
    ntile = counts.shape[0]
    nload = ntile // UNROLL

    def load_counts(c):
        where = pl.ds(c * UNROLL, UNROLL)
        return pltpu.make_async_copy(counts_h.at[where], counts.at[where], sems.at[c])

    loads = [
        pltpu.make_async_copy(dst_h, dst, sems.at[nload]),
        pltpu.make_async_copy(src_h, src, sems.at[nload + 1]),
        pltpu.make_async_copy(feats_h, feats, sems.at[nload + 2]),
    ]
    for load in loads:
        load.start()
    for c in range(nload):
        load_counts(c).start()
    acc[...] = jnp.zeros_like(acc)
    deg[...] = jnp.zeros_like(deg)
    held[:, cols:, :] = jnp.ones((nsrc, rows - cols, tile), BF16)
    for load in loads:
        load.wait()
    for b in range(nsrc):
        held[b, :cols, :] = feats[:, b * tile : (b + 1) * tile]

    def chunk(c, _):
        load_counts(c).wait()
        for u in range(UNROLL):
            t = c * UNROLL + u
            d = dst[t]
            got = lax.dot_general(
                held[src[t]],
                counts[t].astype(F32).astype(BF16),
                (((1,), (1,)), ((), ())),
                preferred_element_type=F32,
            )
            owner, blk = d // per_owner, d % per_owner
            y, r = blk // per_part, blk % per_part
            late_at = SIDE * EARLY + y * (per_part - EARLY) + r - EARLY
            at = jnp.where(r < EARLY, y * EARLY + r, late_at)
            lanes = pl.ds(pl.multiple_of(at * tile, tile), tile)
            acc[owner, :, lanes] += got[:cols]
            deg[owner, :, lanes] += got[cols : cols + 8]
        return _

    lax.fori_loop(0, nload, chunk, 0)
    stores = []
    far_sums[...] = acc[lax.rem(me[0] + 4, owners), :, early:].astype(BF16)
    stores.append((far_sums, late_h[4]))
    stores.append((acc.at[lax.rem(me[0] + 5, owners), :, pl.ds(early, seeds_here - early)], late_h[5]))
    width = short.shape[2]
    for o in range(owners):
        for r in range(short.shape[1]):
            short[o, r : r + 1, :] = deg[o, :1, r * width : (r + 1) * width]
    stores.append((short, deg_h))
    stores.append((acc.at[:, :, pl.ds(0, early)], sums_h))
    for k in (3, 6, 2, 7, 1, 0):
        stores.append((acc.at[lax.rem(me[0] + k, owners), :, pl.ds(early, seeds_here - early)], late_h[k]))
    stores = [pltpu.make_async_copy(p, q, sems.at[i]) for i, (p, q) in enumerate(stores)]
    for store in stores:
        store.start()
    for store in stores:
        store.wait()


def tile_sums(me, dst_block, src_block, feats_t, counts, owners, seeds_here):
    ntile, tile, _ = counts.shape
    cols, sources = feats_t.shape
    early = seeds_here // 8 * EARLY
    outs = [((owners, cols, early), F32)]
    for k in range(owners):
        outs.append(((cols, seeds_here - early), BF16 if k == 4 else F32))
    outs.append(((owners, 8, seeds_here // 8), F32))
    sums, *late, deg = pl.pallas_call(
        tile_kernel,
        in_specs=[pl.BlockSpec(memory_space=pltpu.SMEM)] + [HBM] * 4,
        out_specs=[HBM] * len(outs),
        out_shape=[pltpu.HBM(*o) for o in outs],
        scratch_shapes=[
            pltpu.SMEM((ntile,), jnp.int32),
            pltpu.SMEM((ntile,), jnp.int32),
            pltpu.VMEM((cols, sources), BF16),
            pltpu.VMEM(counts.shape, jnp.int32),
            pltpu.VMEM((owners, cols, seeds_here), F32),
            pltpu.VMEM((owners, 8, seeds_here), F32),
            pltpu.VMEM((sources // tile, cols + 16, tile), BF16),
            pltpu.VMEM((owners, 8, seeds_here // 8), F32),
            pltpu.VMEM((cols, seeds_here - early), BF16),
            pltpu.SemaphoreType.DMA((max(ntile // UNROLL + 3, len(outs)),)),
        ],
        compiler_params=pltpu.CompilerParams(vmem_limit_bytes=40 * 1024 * 1024),
    )(me, *far(dst_block, src_block, feats_t, counts))
    return sums, late, deg


def mean_kernel(total_h, degree_h, send_h, total, degree, send, sems):
    width = send.shape[2]
    lanes = [pl.ds(y * width, width) for y in range(SIDE)]
    first = pltpu.make_async_copy(degree_h, degree, sems.at[0])
    first.start()
    loads = [
        pltpu.make_async_copy(total_h.at[:, lanes[y]], total.at[:, lanes[y]], sems.at[1 + y])
        for y in range(SIDE)
    ]
    for load in loads:
        load.start()
    first.wait()
    stores = []
    for y in range(SIDE):
        loads[y].wait()
        send[y] = (total[:, lanes[y]] / (degree[:, lanes[y]] + 1.0)).astype(BF16)
        for x in range(SIDE):
            i = x * SIDE + y
            store = pltpu.make_async_copy(send.at[y], send_h.at[i], sems.at[1 + SIDE + i])
            store.start()
            stores.append(store)
    for store in stores:
        store.wait()


def mean_rows(total, degree):
    cols, n = total.shape
    send = (SIDE, cols, n // SIDE)
    return pl.pallas_call(
        mean_kernel,
        in_specs=[HBM, HBM],
        out_specs=HBM,
        out_shape=pltpu.HBM((SIDE * SIDE, *send[1:]), BF16),
        scratch_shapes=[
            pltpu.VMEM(total.shape, F32),
            pltpu.VMEM(degree.shape, F32),
            pltpu.VMEM(send, BF16),
            pltpu.SemaphoreType.DMA((1 + SIDE + SIDE * SIDE,)),
        ],
        compiler_params=pltpu.CompilerParams(vmem_limit_bytes=16 * 1024 * 1024),
    )(*far(total), degree)


def late_kernel(ws_h, seeds_h, wn_h, means_h, hid_h, pre_h, ws, seeds, wn, means, hid, pre, sems):
    early = pre.shape[1]
    pairs = ((ws_h, ws), (seeds_h, seeds), (wn_h, wn), (means_h, means))
    loads = [pltpu.make_async_copy(p, q, sems.at[i]) for i, (p, q) in enumerate(pairs)]
    for load in loads:
        load.start()
    for load in loads:
        load.wait()
    total = jnp.dot(ws[...], seeds[...], preferred_element_type=F32)
    pre[...] = total[:, :early]
    total = total[:, early:] + jnp.dot(wn[...], means[...], preferred_element_type=F32)
    hid[...] = jnp.maximum(total, 0.0).astype(BF16)
    lanes = (slice(None), pl.ds(early, hid.shape[1]))
    stores = [
        pltpu.make_async_copy(hid, hid_h.at[lanes], sems.at[4]),
        pltpu.make_async_copy(pre, pre_h, sems.at[5]),
    ]
    for store in stores:
        store.start()
    for store in stores:
        store.wait()


def late_rows(ws_t, seeds, wn_t, means):
    hcols, _ = ws_t.shape
    rows, late = seeds.shape[1], means.shape[1]
    return pl.pallas_call(
        late_kernel,
        in_specs=[HBM] * 3 + [pl.BlockSpec(memory_space=pl.ANY)],
        out_specs=[HBM] * 2,
        out_shape=[pltpu.HBM((hcols, rows), BF16), pltpu.HBM((hcols, rows - late), F32)],
        scratch_shapes=[pltpu.VMEM(a.shape, BF16) for a in (ws_t, seeds, wn_t, means)]
        + [
            pltpu.VMEM((hcols, late), BF16),
            pltpu.VMEM((hcols, rows - late), F32),
            pltpu.SemaphoreType.DMA((6,)),
        ],
        compiler_params=pltpu.CompilerParams(vmem_limit_bytes=32 * 1024 * 1024),
    )(*far(ws_t, seeds, wn_t), means)


def layer_kernel(wn_h, means_h, pre_h, cot_h, late_h, before_h, seeds_h, hid_h, grad_h, *refs):
    wn, means, pre, cot, seeds, hid, grad, sems = refs
    early, rows = pre.shape[1], cot.shape[1]
    first = (slice(None), pl.ds(0, early))
    rest = (slice(None), pl.ds(early, rows - early))
    pairs = (
        (wn_h, wn),
        (means_h, means.at[first]),
        (pre_h, pre),
        (cot_h, cot),
        (before_h.at[rest], hid.at[rest]),
        (seeds_h, seeds),
        (late_h, means.at[rest]),
    )
    loads = [pltpu.make_async_copy(p, q, sems.at[i]) for i, (p, q) in enumerate(pairs)]
    for load in loads:
        load.start()
    for load in loads[:3]:
        load.wait()
    total = pre[...] + jnp.dot(wn[...], means[first], preferred_element_type=F32)
    hid[first] = jnp.maximum(total, 0.0).astype(BF16)
    stores = [pltpu.make_async_copy(hid.at[first], hid_h.at[first], sems.at[7])]
    stores[0].start()
    for load in loads[3:]:
        load.wait()
    dpre = jnp.where(hid[...] > 0, cot[...], jnp.zeros_like(cot))
    dims = (((1,), (1,)), ((), ()))
    nf, cols = grad.shape[0], grad.shape[1] // 2
    for j, x in enumerate((seeds, means)):
        at = j * cols
        g = lax.dot_general(x[...], dpre, dims, preferred_element_type=F32).astype(BF16)
        for i in range(nf):
            grad[i, at : at + cols, :] = g[i * cols : (i + 1) * cols]
        where = (slice(None), pl.ds(at, cols), slice(None))
        store = pltpu.make_async_copy(grad.at[where], grad_h.at[where], sems.at[8 + j])
        store.start()
        stores.append(store)
    for store in stores:
        store.wait()


def layer(wn_t, means, pre, cot, late, before, seeds, nf):
    hcols, rows = cot.shape
    depth, early = means.shape
    grad = (nf, 2 * depth // nf, hcols)
    anywhere = pl.BlockSpec(memory_space=pl.ANY)
    return pl.pallas_call(
        layer_kernel,
        in_specs=[HBM, anywhere] + [HBM] * 2 + [anywhere] + [HBM] * 2,
        out_specs=[HBM] * 2,
        out_shape=[pltpu.HBM((hcols, rows), BF16), pltpu.HBM(grad, BF16)],
        scratch_shapes=[
            pltpu.VMEM((hcols, depth), BF16),
            pltpu.VMEM((depth, rows), BF16),
            pltpu.VMEM((hcols, early), F32),
            pltpu.VMEM((hcols, rows), BF16),
            pltpu.VMEM((depth, rows), BF16),
            pltpu.VMEM((hcols, rows), BF16),
            pltpu.VMEM(grad, BF16),
            pltpu.SemaphoreType.DMA((10,)),
        ],
        input_output_aliases={5: 0},
        compiler_params=pltpu.CompilerParams(vmem_limit_bytes=40 * 1024 * 1024),
    )(*far(wn_t), means, *far(pre, cot), late, *far(before, seeds))


def shards(seed_feats, src_feats, counts, dst_block, src_block, w_self, w_neigh, cotangent):
    seeds_here, cols = seed_feats.shape
    ng = lax.axis_size("group")
    nf = lax.axis_size("feat")
    part = seeds_here // SIDE
    ccols = cotangent.shape[1]
    hcols = SIDE * ccols
    f = lax.axis_index("feat")
    fx, fy = f // SIDE, f % SIDE

    def shift_y(a, k):
        return lax.ppermute(
            a, "feat", [(i, i // SIDE * SIDE + (i % SIDE + k) % SIDE) for i in range(nf)]
        )

    def shift_z(a, k):
        return lax.ppermute(a, "group", [(i, (i + k) % ng) for i in range(ng)])

    def plus(a, k):
        return (a.astype(F32) + late[k]).astype(BF16)

    def meet(*arrays):
        return lax.optimization_barrier(arrays)

    with jax.named_scope("tile_sums"):
        me = lax.axis_index("group")[None].astype(jnp.int32)
        sums, late, deg = tile_sums(
            me, dst_block, src_block, src_feats.T, counts, ng, seeds_here
        )

    with jax.named_scope("neighbour_sum"):
        total = lax.psum_scatter(
            sums.reshape(ng * cols, -1), "group", scatter_dimension=0, tiled=True
        )

    with jax.named_scope("weights"):
        ws_t = lax.dynamic_slice_in_dim(w_self, fx * hcols, hcols, 1).T
        wn_t = lax.dynamic_slice_in_dim(w_neigh, fx * hcols, hcols, 1).T

    with jax.named_scope("hop_1"):
        up = shift_z(late[4], 1)
        down = shift_z(late[5], -1)
        up, down, seed_t, cot_t = meet(up, down, seed_feats.T, cotangent.T)

    with jax.named_scope("degree"):
        degree = jnp.sum(lax.all_to_all(deg, "group", 0, 0), axis=0).reshape(1, seeds_here)

    with jax.named_scope("seed_rows"):
        send = seed_t.reshape(cols, SIDE, part).transpose(1, 0, 2)
        send = jnp.broadcast_to(send[None], (SIDE, SIDE, cols, part)).reshape(nf, cols, part)
        seeds = lax.all_to_all(send, "feat", 0, 0).reshape(nf * cols, part)

    with jax.named_scope("hop_2"):
        up = shift_z(plus(up, 3), 1)
        down = shift_z(down + late[6], -1)
        up, down, degree = meet(up, down, degree)

    with jax.named_scope("cotangent_rows"):
        cot = jnp.zeros((SIDE, ccols, part), BF16)
        for k in range(SIDE):
            piece = lax.dynamic_slice_in_dim(cot_t, (fy + k) % SIDE * part, part, 1)
            piece = shift_y(piece, k) if k else piece
            cot = lax.dynamic_update_slice(cot, piece[None], ((fy - k) % SIDE, 0, 0))
        cot = cot.reshape(hcols, part)

    with jax.named_scope("hop_3"):
        up = shift_z(plus(up, 2), 1)
        down = shift_z(down + late[7], -1)
        up, down, cot = meet(up, down, cot)

    with jax.named_scope("hop_4"):
        up = shift_z(plus(up, 1), 1)
        total2, seeds = meet(late[0] + up.astype(F32) + down, seeds)

    early = total.shape[1]
    means = []
    for x, lo, hi in ((total2, early, seeds_here), (total, 0, early)):
        with jax.named_scope("mean_rows_%d" % lo):
            send = mean_rows(x, degree[:, lo:hi])
            means.append(lax.all_to_all(send, "feat", 0, 0).reshape(nf * cols, -1))

    with jax.named_scope("layer"):
        hid, pre = late_rows(ws_t, seeds, wn_t, means[0])
        hid, both = layer(wn_t, means[1], pre, cot, means[0], hid, seeds, nf)

    with jax.named_scope("grads"):
        got = lax.all_to_all(both, "feat", 0, 0).astype(F32)
        got = jnp.sum(got.reshape(SIDE, SIDE, 2 * cols, hcols), axis=1)
        got = got.reshape(SIDE, 2 * cols, 2, hcols // 2).transpose(0, 2, 1, 3)
        got = got.reshape(ng, 2 * cols, hcols // 2).astype(BF16)
        got, hid = lax.optimization_barrier((got, hid))
        got = jnp.sum(lax.all_to_all(got, "group", 0, 0).astype(F32), axis=0)

    with jax.named_scope("hidden_columns"):
        hid4 = hid.reshape(SIDE, ccols, part)
        pieces = []
        for k in range(SIDE):
            piece = lax.dynamic_index_in_dim(hid4, (fy + k) % SIDE, 0, keepdims=False)
            pieces.append(shift_y(piece, k) if k else piece)
        got, *pieces = lax.optimization_barrier((got, *pieces))
        out = jnp.zeros((ccols, seeds_here), BF16)
        for k in range(SIDE):
            out = lax.dynamic_update_slice(out, pieces[k], (0, (fy - k) % SIDE * part))
    return (out.T, got[:cols], got[cols:])


def solution(mesh):
    in_specs = (
        P(("rep", "group"), "feat"),
        P(("rep", "group"), "feat"),
        P(("rep", "group"), None, None),
        P(("rep", "group")),
        P(("rep", "group")),
        P(),
        P(),
        P(("rep", "group"), "feat"),
    )
    out_specs = (
        P(("rep", "group"), "feat"),
        P(("rep", "feat"), "group"),
        P(("rep", "feat"), "group"),
    )
    return jax.shard_map(shards, mesh=mesh, in_specs=in_specs, out_specs=out_specs, check_vma=False)
```
